512 devices in a mesh: row: 128 (over z, y, core), col: 4 (over x).
Axes of the slice: x: 4, y: 4, z: 16, core: 2. Of those that a mesh axis runs over, the one named last changes fastest.
Arguments:
- left_values: bfloat16 [3, 131072, 512], P(None, 'row', 'col'), may hold values from -40 to 40
- left_pattern: int32 [3, 1024, 4], P(None, 'row', 'col'), may hold values from 0 to 1, as said below
- right_values: bfloat16 [131072, 2048], P('row', 'col'), may hold values from -0.25 to 0.25
- right_pattern: int32 [1024, 16], P('row', 'col'), may hold values from 0 to 1, as said below
Outputs:
- normalized: float32 [131072, 2048], P('row', 'col')
The draws below stay inside these ranges and needn't reach their ends.
Inputs may be any that keep to these rules, and one draw needn't show every extreme that they name: `left_pattern`: in each panel, the 8 tiles of one device (aligned blocks of 8 tile rows, one tile column) hold 1 to 6 occupied tiles; in every panel some block of 8 tile rows holds 6 in each of its 4 tile columns. `right_pattern`: in every aligned block of 8 tile rows, each tile column has at least one occupied tile among the block's first 4 tile rows.
All inputs are finite; a program needn't handle non-finite values.
Results may differ from the reference program's by a relative error of at most 0.0003.
Values may be sent and summed in bfloat16 or wider, within the bound.
A program may use at most 64 MiB of HBM per device.

```python
import math
import jax
import jax.numpy as jnp
from jax import lax

TILE = 128
TR = 8
SECTIONS = 3
CAP_L = 6
KS = 4
INNER = 512
ROOT_STEP = 42
ROW_TILES = 1024
ROWS = 131072
SLAB_TILES = 16
SLAB = 2048


def draw_left_pattern(key, part):
    key = jax.random.fold_in(key, 5)
    first_key, second_key, third_key = jax.random.split(key, 3)
    blocks = ROW_TILES // TR
    counts = jax.random.randint(first_key, (SECTIONS, blocks, KS), 1, CAP_L + 1)
    full = jax.random.randint(second_key, (SECTIONS, 1, 1), 0, blocks)
    counts = jnp.where(jnp.arange(blocks)[None, :, None] == full, CAP_L, counts)
    random_keys = jax.random.randint(third_key, (SECTIONS, blocks, TR, KS), 0, 1 << 20)
    score = random_keys * TR + jnp.arange(TR)[None, None, :, None]
    rank = jnp.argsort(jnp.argsort(score, axis=2, stable=True), axis=2, stable=True)
    occupied = (rank < counts[:, :, None, :]).astype(jnp.int32)
    return occupied.reshape(SECTIONS, ROW_TILES, KS)


def draw_right_pattern(key, part):
    key = jax.random.fold_in(key, 7)
    first_key, second_key = jax.random.split(key, 2)
    blocks = ROW_TILES // TR
    coin = jax.random.randint(first_key, (blocks, TR, SLAB_TILES), 0, 2)
    pick = jax.random.randint(second_key, (blocks, 1, SLAB_TILES), 0, KS)
    forced = (jnp.arange(TR)[None, :, None] == pick).astype(jnp.int32)
    return jnp.maximum(coin, forced).reshape(ROW_TILES, SLAB_TILES)


def draw_left_values(key, part):
    key = jax.random.fold_in(key, 11)
    first_key, second_key = jax.random.split(key, 2)
    place = jnp.arange(ROWS, dtype=jnp.float32) / ROWS
    base = jnp.clip(jax.random.normal(first_key, (SECTIONS, ROWS, INNER), jnp.float32), -6.0, 6.0)
    ramp = jnp.sqrt(1.0 + 2.0 * place)
    spread = jnp.exp(0.5 * math.log(10.0) * jax.random.uniform(second_key, (ROWS,), jnp.float32))
    values = base * (ramp * spread)[None, :, None]
    return jnp.clip(values, -40.0, 40.0).astype(jnp.bfloat16)


def shard_levels(key, extent, cuts, low, top_value):
    def one(dim, parts):
        heights = jax.random.uniform(jax.random.fold_in(jax.random.fold_in(key, 6), dim), (parts,), jnp.float32, low / len(cuts), top_value / len(cuts))
        return jnp.repeat(jnp.exp(heights), extent[dim] // parts).reshape((-1,) + (1,) * (len(extent) - dim - 1))

    level = one(*cuts[0])
    for cut in cuts[1:]:
        level = level * one(*cut)
    return level


def normal_values(own_key, shape, scale, most, pieces=(), kind=jnp.bfloat16):
    entries = scale * jax.random.normal(own_key, shape, jnp.float32)
    if pieces:
        entries = entries * shard_levels(own_key, shape, pieces, -0.22, 0.18)
    return jnp.clip(entries, -most, most).astype(kind)


def setup_inputs(seed: int = 0) -> dict:
    arg_keys = jax.random.split(jax.random.key(seed), 5)
    return {
        "left_values": draw_left_values(jax.random.fold_in(arg_keys[4], 71), 0),
        "left_pattern": draw_left_pattern(jax.random.fold_in(arg_keys[4], 71), 0),
        "right_values": normal_values(arg_keys[2], (ROWS, SLAB), INNER ** -0.5, 0.25, ((0, 128), (1, 4))),
        "right_pattern": draw_right_pattern(jax.random.fold_in(arg_keys[4], 71), 0),
    }


def expand(pattern, tile_size):
    return jnp.repeat(jnp.repeat(pattern, tile_size, axis=1), tile_size, axis=2)


def expand_plane(pattern, tile_size):
    return jnp.repeat(jnp.repeat(pattern, tile_size, axis=0), tile_size, axis=1)


def reference(left_values, left_pattern, right_values, right_pattern):
    panels = []
    for section in range(SECTIONS):
        first_tile = section * ROOT_STEP * TR
        values = right_values[first_tile * TILE:first_tile * TILE + INNER]
        tiles = right_pattern[first_tile:first_tile + KS]
        panels.append(values * expand_plane(tiles, TILE).astype(jnp.bfloat16))
    right = jnp.stack(panels)
    block_rows = TR * TILE

    def block_squares(block_index):
        rows = lax.dynamic_slice_in_dim(left_values, block_index * block_rows, block_rows, 1)
        tiles = lax.dynamic_slice_in_dim(left_pattern, block_index * TR, TR, 1)
        masked = rows * expand(tiles, TILE).astype(jnp.bfloat16)
        total = jnp.zeros((block_rows, SLAB), jnp.float32)
        for section in range(SECTIONS):
            total = total + jnp.dot(masked[section], right[section], preferred_element_type=jnp.float32)
        return total * total

    inflated = lax.map(block_squares, jnp.arange(ROW_TILES // TR, dtype=jnp.int32))
    column_total = jnp.sum(inflated, axis=(0, 1))
    normalized = inflated * (ROWS / column_total)
    return normalized.reshape(ROWS, SLAB)
```

```python
import jax
import jax.numpy as jnp
from jax import lax
from jax.experimental import pallas as pl
from jax.experimental.pallas import tpu as pltpu
from jax.sharding import PartitionSpec as P

TILE = 128
TR = 8
SLOTS = 6
HALF = SLOTS // 2
S = 3
NX, NZ, NG = 4, 16, 8
NY = 4
STEP = 42
COLS = 512
PIECE = 64
FIRST = S * 3 * TILE
MESH = pl.DeviceIdType.MESH
ORDER = (0, 1, 3, 2)


def base(s, q):
    return s * 3 * TILE + q * TILE if q < 3 else FIRST + s * TILE


def free_slots(pattern):
    first, last = SLOTS - 1, 0
    for i in range(SLOTS):
        last = jnp.where(pattern[i] == 0, i, last)
        first = jnp.where(pattern[SLOTS - 1 - i] == 0, SLOTS - 1 - i, first)
    return first, last


def kernel(left_hbm, pat, right_hbm, rpat, out, scale, own, pack, from_next, from_prev, from_far, pats, raw, root,
           left, right, mine, group, part, column, psend, precv, xsend, xrecv, rootsend, ownrecv, treesend, ysend, yrecv,
           csend, crecv, gsend, grecv, zsend, zrecv, load):
    r, x = lax.axis_index("row"), lax.axis_index("col")
    z, g = r // NG, r % NG
    y, c = g // 2, g % 2

    def at_x(d):
        return (r, (x + d) % NX)

    def at_z(d):
        return (((z + d) % NZ) * NG + g, x)

    def at_y(d):
        return (z * NG + ((y + d) % NY) * 2 + c, x)

    def at_g(d):
        return (z * NG + (g + d) % NG, x)

    sibling = (z * NG + y * 2 + 1 - c, x)

    def copy(src, dst, send, recv, to):
        return pltpu.make_async_remote_copy(src_ref=src, dst_ref=dst, send_sem=send, recv_sem=recv, device_id=to, device_id_type=MESH)

    barrier = pltpu.get_barrier_semaphore()
    peers = [at_x(d) for d in range(1, NX)] + [at_g(d) for d in range(1, NG)] + [at_z(d) for d in range(1, NZ)]
    for peer in peers:
        pl.semaphore_signal(barrier, inc=1, device_id=peer, device_id_type=MESH)

    loads = [pltpu.make_async_copy(left_hbm.at[s], own[s], load.at[s]) for s in range(S)]
    for cp in loads:
        cp.start()
    is_root = jnp.logical_and(r % STEP == 0, r // STEP < S)
    load_right = pltpu.make_async_copy(right_hbm.at[pl.ds(0, NX * TILE)], raw, load.at[S])

    def piece(s, p):
        return s * 3 * TILE + p * PIECE + (p // 6) * (FIRST + s * TILE - 6 * PIECE - s * 3 * TILE)

    def piece_of(s, p):
        return right.at[pl.ds(pl.multiple_of(piece(s, p), PIECE), PIECE)]

    @pl.when(is_root)
    def _():
        load_right.start()
        load_right.wait()
        for q, d in enumerate(ORDER):
            k = (x + d) % NX
            for j in range(COLS // TILE):
                tile = raw[pl.ds(pl.multiple_of(k * TILE, TILE), TILE), pl.ds(j * TILE, TILE)]
                root[pl.ds(q * TILE, TILE), pl.ds(j * TILE, TILE)] = jnp.where(rpat[k, j] != 0, tile, jnp.zeros_like(tile))

    own_pattern = [[pat[s, i] for i in range(TR)] for s in range(S)]
    for s in range(S):
        first, last = free_slots(own_pattern[s])
        loads[s].wait()
        for t in range(SLOTS):
            at = jnp.where(jnp.logical_and(own_pattern[s][TR - 2] != 0, first == t), TR - 2, t)
            at = jnp.where(jnp.logical_and(own_pattern[s][TR - 1] != 0, last == t), TR - 1, at)
            pack[s, t] = own[s][at]

    pl.semaphore_wait(barrier, len(peers))

    my_panel = r // STEP
    root_copies = [
        copy(root.at[pl.ds(pl.multiple_of(((g + d) % NG) * PIECE, PIECE), PIECE)], piece_of(my_panel, (g + d) % NG),
             rootsend.at[d - 1], ownrecv.at[my_panel], at_g(d))
        for d in range(1, NG)
    ]

    @pl.when(is_root)
    def _():
        for cp in root_copies:
            cp.start()
        start = pl.multiple_of(piece(my_panel, g), PIECE)
        right[pl.ds(start, PIECE)] = root[pl.ds(pl.multiple_of(g * PIECE, PIECE), PIECE)]

    pattern_copies = [copy(pat, pats[d], psend.at[d], precv.at[d], at_x(NX - d)) for d in range(1, NX)]
    for cp in pattern_copies:
        cp.start()
    halves = [pl.ds(0, HALF), pl.ds(HALF, HALF)]
    to_next = [[copy(pack.at[s, halves[h]], from_prev[s].at[halves[h]], xsend.at[0, s, h], xrecv.at[0, s, h], at_x(1)) for h in range(2)] for s in range(S)]
    to_prev = [[copy(pack.at[s, halves[h]], from_next[s].at[halves[h]], xsend.at[1, s, h], xrecv.at[1, s, h], at_x(NX - 1)) for h in range(2)] for s in range(S)]
    for h in range(2):
        for s in range(S):
            to_next[s][h].start()
            to_prev[s][1 - h].start()
    far_next = [copy(from_prev[s].at[halves[0]], from_far[s].at[halves[0]], xsend.at[2, s, 0], xrecv.at[2, s, 0], at_x(1)) for s in range(S)]
    far_prev = [copy(from_next[s].at[halves[1]], from_far[s].at[halves[1]], xsend.at[2, s, 1], xrecv.at[2, s, 1], at_x(NX - 1)) for s in range(S)]

    own_copies = [copy(piece_of(s, g), piece_of(s, g), rootsend.at[0], ownrecv.at[s], at_g(1)) for s in range(S)]
    far = 2 - c * 4 + NZ
    zero = [STEP * s // NG for s in range(S)]
    for s in range(S):
        hub_copies = [copy(piece_of(s, g), piece_of(s, g), treesend.at[i], ownrecv.at[s], at_z(d)) for i, d in enumerate((8, 4, 12))]

        @pl.when(z == zero[s])
        def _():
            @pl.when(g != STEP * s % NG)
            def _():
                own_copies[s].wait_recv()

            for cp in hub_copies:
                cp.start()

    for s in range(S):
        rel = (z - zero[s] + NZ) % NZ
        leaf_copies = [copy(piece_of(s, g), piece_of(s, g), treesend.at[3 + i], ownrecv.at[s], at_z(d)) for i, d in enumerate((far, 1, NZ - 1))]

        @pl.when(rel % 4 == 0)
        def _():
            @pl.when(rel != 0)
            def _():
                own_copies[s].wait_recv()

            for cp in leaf_copies:
                cp.start()

    y_copies, c_copies = [], []
    for s in range(S):
        rel = (z - zero[s] + NZ) % NZ

        @pl.when(rel % 4 != 0)
        def _():
            own_copies[s].wait_recv()

        y_copies.append([copy(piece_of(s, g), piece_of(s, g), ysend.at[s, d - 1], yrecv.at[s, d - 1], at_y(d)) for d in range(1, NY)])
        c_copies.append([copy(piece_of(s, (g + NG - 2 * d) % NG), piece_of(s, (g + NG - 2 * d) % NG), csend.at[s, d], crecv.at[s, d], sibling) for d in range(NY)])
        for d in (2, 1, 3):
            y_copies[s][d - 1].start()
        c_copies[s][0].start()

    def place(s, q, pattern, tiles, low, high):
        for i, tile in zip((0, 1, 2, 3, 4, 5, 6, 7), (0, 1, 2, 3, 4, 5, low, high)):
            value = tiles[tile]
            left[pl.ds(i * TILE, TILE), pl.ds(base(s, q), TILE)] = jnp.where(pattern[i] != 0, value, jnp.zeros_like(value))

    for s in range(S):
        place(s, 0, own_pattern[s], own[s], TR - 2, TR - 1)

    for s in range(S):
        to_next[s][0].wait_recv()
        far_next[s].start()
        to_prev[s][1].wait_recv()
        far_prev[s].start()

    for s in range(S):
        for d in (1, 3, 2):
            y_copies[s][d - 1].wait_recv()
            c_copies[s][d].start()

    for cp in pattern_copies:
        cp.wait_recv()

    def received(s, q, tiles):
        pattern = [pats[ORDER[q]][s, i] for i in range(TR)]
        first, last = free_slots(pattern)
        place(s, q, pattern, tiles, first, last)

    for s in range(S):
        to_next[s][1].wait_recv()
        to_prev[s][0].wait_recv()
        received(s, 1, from_next[s])
        received(s, 2, from_prev[s])

    for s in range(S):
        for d in range(NY):
            c_copies[s][d].wait_recv()

    for n in range(2):
        cols = pl.ds(n * 256, 256)
        out[:, cols] = jnp.dot(left[:, :FIRST], right[:FIRST, cols], preferred_element_type=jnp.float32)

    for s in range(S):
        far_next[s].wait_recv()
        far_prev[s].wait_recv()
        received(s, 3, from_far[s])

    for n in range(2):
        cols = pl.ds(n * 256, 256)
        total = out[:, cols] + jnp.dot(left[:, FIRST:], right[FIRST:, cols], preferred_element_type=jnp.float32)
        total = total * total
        out[:, cols] = total
        mine[:, cols] = jnp.sum(total, axis=0, keepdims=True)

    g_copies = [copy(mine, group.at[d - 1], gsend.at[d - 1], grecv.at[d - 1], at_g(d)) for d in range(1, NG)]
    for cp in g_copies:
        cp.start()
    for cp in g_copies:
        cp.wait_recv()
    part[...] = mine[...] + jnp.sum(group[...], axis=0)
    z_copies = [copy(part, column.at[d - 1], zsend.at[d - 1], zrecv.at[d - 1], at_z(d)) for d in range(1, NZ)]
    for cp in z_copies:
        cp.start()
    for cp in z_copies:
        cp.wait_recv()
    rows_total = TR * TILE * NZ * NG
    scale[...] = rows_total / (part[...] + jnp.sum(column[...], axis=0))

    @pl.when(is_root)
    def _():
        for cp in root_copies:
            cp.wait_send()

    for s in range(S):
        waiter = [copy(piece_of(s, g), piece_of(s, g), treesend.at[i], ownrecv.at[s], at_z(1)) for i in range(6)]

        @pl.when(z == zero[s])
        def _():
            for cp in waiter[:3]:
                cp.wait_send()

        @pl.when((z - zero[s] + NZ) % NZ % 4 == 0)
        def _():
            for cp in waiter[3:]:
                cp.wait_send()

    flat = pattern_copies + far_next + far_prev + g_copies + z_copies
    for group_of in to_next + to_prev + y_copies + c_copies:
        flat = flat + group_of
    for cp in flat:
        cp.wait_send()


def on_device(left_values, left_pattern, right_values, right_pattern):
    tiles = left_values.reshape(S, TR, TILE, TILE)
    pattern = left_pattern.reshape(S, TR)
    rows = TR * TILE
    dma = pltpu.SemaphoreType.DMA
    box = lambda n: tuple(pltpu.VMEM((n, TILE, TILE), jnp.bfloat16) for _ in range(S))
    any_space, smem, vmem = (pl.BlockSpec(memory_space=m) for m in (pl.ANY, pltpu.SMEM, pltpu.VMEM))
    squares, scale = pl.pallas_call(
        kernel,
        out_shape=(pltpu.VMEM((rows, COLS), jnp.float32), pltpu.VMEM((1, COLS), jnp.float32)),
        in_specs=[any_space, smem, any_space, smem],
        out_specs=(vmem, vmem),
        scratch_shapes=[
            box(TR),
            pltpu.VMEM((S, SLOTS, TILE, TILE), jnp.bfloat16),
            box(SLOTS), box(SLOTS), box(SLOTS),
            tuple(pltpu.SMEM((S, TR), jnp.int32) for _ in range(NX)),
            pltpu.VMEM((NX * TILE, COLS), jnp.bfloat16),
            pltpu.VMEM((NX * TILE, COLS), jnp.bfloat16),
            pltpu.VMEM((rows, S * NX * TILE), jnp.bfloat16),
            pltpu.VMEM((S * NX * TILE, COLS), jnp.bfloat16),
            pltpu.VMEM((1, COLS), jnp.float32),
            pltpu.VMEM((NG - 1, 1, COLS), jnp.float32),
            pltpu.VMEM((1, COLS), jnp.float32),
            pltpu.VMEM((NZ - 1, 1, COLS), jnp.float32),
            dma((NX,)), dma((NX,)),
            dma((3, S, 2)), dma((3, S, 2)),
            dma((NG - 1,)), dma((S,)), dma((6,)),
            dma((S, NY - 1)), dma((S, NY - 1)),
            dma((S, NY)), dma((S, NY)),
            dma((NG - 1,)), dma((NG - 1,)),
            dma((NZ - 1,)), dma((NZ - 1,)),
            dma((S + 1,)),
        ],
        compiler_params=pltpu.CompilerParams(collective_id=0, has_side_effects=True, vmem_limit_bytes=48 * 1024 * 1024),
    )(tiles, pattern, right_values, right_pattern)
    return squares * scale


def solution(mesh):
    in_specs = (P(None, "row", "col"), P(None, "row", "col"), P("row", "col"), P("row", "col"))
    out_specs = P("row", "col")
    return jax.shard_map(
        on_device, mesh=mesh, in_specs=in_specs, out_specs=out_specs, check_vma=False
    )
```

```python
import jax
import jax.numpy as jnp
from jax import lax
from jax.experimental import pallas as pl
from jax.experimental.pallas import tpu as pltpu
from jax.sharding import PartitionSpec as P

TILE = 128
TR = 8
SLOTS = 6
HALF = SLOTS // 2
S = 3
NX, NZ, NG = 4, 16, 8
NY = 4
STEP = 42
COLS = 512
PIECE = 64
FIRST = S * 3 * TILE
MESH = pl.DeviceIdType.MESH
ORDER = (0, 1, 3, 2)


def base(s, q):
    return s * 3 * TILE + q * TILE if q < 3 else FIRST + s * TILE


def free_slots(pattern):
    first, last = SLOTS - 1, 0
    for i in range(SLOTS):
        last = jnp.where(pattern[i] == 0, i, last)
        first = jnp.where(pattern[SLOTS - 1 - i] == 0, SLOTS - 1 - i, first)
    return first, last


def kernel(left_hbm, pat, right_hbm, rpat, out, scale, own, pack, from_next, from_prev, from_far, pats, raw, root, spare,
           left, right, mine, other, pair, chips, part, column, psend, precv, xsend, xrecv, rootsend, sparerecv, ownrecv, treesend,
           ysend, yrecv, csend, crecv, asend, arecv, zsend, zrecv, load, known):
    r, x = lax.axis_index("row"), lax.axis_index("col")
    z, g = r // NG, r % NG
    y, c = g // 2, g % 2

    def at_x(d):
        return (r, (x + d) % NX)

    def at_z(d):
        return (((z + d + NZ) % NZ) * NG + g, x)

    def at_y(d):
        return (z * NG + ((y + d) % NY) * 2 + c, x)

    sibling = (z * NG + y * 2 + 1 - c, x)

    def copy(src, dst, send, recv, to):
        return pltpu.make_async_remote_copy(src_ref=src, dst_ref=dst, send_sem=send, recv_sem=recv, device_id=to, device_id_type=MESH)

    barrier = pltpu.get_barrier_semaphore()
    peers = [at_x(d) for d in range(1, NX)] + [at_y(d) for d in range(1, NY)] + [sibling] + [at_z(d) for d in (1, NZ - 1)]
    for peer in peers:
        pl.semaphore_signal(barrier, inc=1, device_id=peer, device_id_type=MESH)

    loads = [pltpu.make_async_copy(left_hbm.at[s], own[s], load.at[s]) for s in range(S)]
    for cp in loads:
        cp.start()
    is_root = jnp.logical_and(r % STEP == 0, r // STEP < S)
    load_right = pltpu.make_async_copy(right_hbm.at[pl.ds(0, NX * TILE)], raw, load.at[S])

    def piece(s, p):
        return s * 3 * TILE + p * PIECE + (p // 6) * (FIRST + s * TILE - 6 * PIECE - s * 3 * TILE)

    def piece_of(s, p):
        return right.at[pl.ds(pl.multiple_of(piece(s, p), PIECE), PIECE)]

    @pl.when(is_root)
    def _():
        load_right.start()
        load_right.wait()
        for q, d in enumerate(ORDER):
            k = (x + d) % NX
            for j in range(COLS // TILE):
                tile = raw[pl.ds(pl.multiple_of(k * TILE, TILE), TILE), pl.ds(j * TILE, TILE)]
                root[pl.ds(q * TILE, TILE), pl.ds(j * TILE, TILE)] = jnp.where(rpat[j, k] != 0, tile, jnp.zeros_like(tile))

    own_pattern = [[pat[s, 0, i] for i in range(TR)] for s in range(S)]
    for s in range(S):
        first, last = free_slots(own_pattern[s])
        loads[s].wait()
        for t in range(SLOTS):
            at = jnp.where(jnp.logical_and(own_pattern[s][TR - 2] != 0, first == t), TR - 2, t)
            at = jnp.where(jnp.logical_and(own_pattern[s][TR - 1] != 0, last == t), TR - 1, at)
            pack[s, t] = own[s][at]

    pl.semaphore_wait(barrier, len(peers))

    def wider(step):
        for to in (1 << step, NZ - (1 << step)):
            pl.semaphore_signal(known.at[step], inc=1, device_id=at_z(to), device_id_type=MESH)

    wider(0)

    my_panel = r // STEP

    def of_root(p):
        return root.at[pl.ds(pl.multiple_of(p * PIECE, PIECE), PIECE)]

    root_copies = []
    for d in range(1, NY):
        p = (g + 2 * d) % NG
        root_copies.append(copy(of_root(p), piece_of(my_panel, p), rootsend.at[2 * d - 2], ownrecv.at[my_panel], at_y(d)))
        root_copies.append(copy(of_root((p + 1) % NG), spare, rootsend.at[2 * d - 1], sparerecv.at[0], at_y(d)))
    root_copies.append(copy(of_root(g + 1 - 2 * c), piece_of(my_panel, g + 1 - 2 * c), rootsend.at[6], ownrecv.at[my_panel], sibling))

    @pl.when(is_root)
    def _():
        for i in (3, 6, 1, 5, 2, 0, 4):
            root_copies[i].start()
        start = pl.multiple_of(piece(my_panel, g), PIECE)
        right[pl.ds(start, PIECE)] = root[pl.ds(pl.multiple_of(g * PIECE, PIECE), PIECE)]

    pattern_copies = [copy(pat, pats[d], psend.at[d], precv.at[d], at_x(NX - d)) for d in range(1, NX)]
    for cp in pattern_copies:
        cp.start()
    halves = [pl.ds(0, HALF), pl.ds(HALF, HALF)]
    to_next = [[copy(pack.at[s, halves[h]], from_prev[s].at[halves[h]], xsend.at[0, s, h], xrecv.at[0, s, h], at_x(1)) for h in range(2)] for s in range(S)]
    to_prev = [[copy(pack.at[s, halves[h]], from_next[s].at[halves[h]], xsend.at[1, s, h], xrecv.at[1, s, h], at_x(NX - 1)) for h in range(2)] for s in range(S)]
    for s, h in ((0, 0), (1, 0), (2, 0), (0, 1)):
        to_next[s][h].start()
        to_prev[s][1 - h].start()
    far_next = [copy(from_prev[s].at[halves[0]], from_far[s].at[halves[0]], xsend.at[2, s, 0], xrecv.at[2, s, 0], at_x(1)) for s in range(S)]
    far_prev = [copy(from_next[s].at[halves[1]], from_far[s].at[halves[1]], xsend.at[2, s, 1], xrecv.at[2, s, 1], at_x(NX - 1)) for s in range(S)]

    def along_z(s, send, d):
        return copy(piece_of(s, g), piece_of(s, g), send, ownrecv.at[s], at_z(d))

    zero = [STEP * s // NG for s in range(S)]
    for s in range(S):
        own_copy = along_z(s, treesend.at[0], 4)
        spare_copy = copy(spare, piece_of(s, g + 1 - 2 * c), rootsend.at[6], ownrecv.at[s], sibling)
        spare_wait = copy(spare, spare, rootsend.at[6], sparerecv.at[0], sibling)

        @pl.when(z == zero[s])
        def _():
            @pl.when(jnp.logical_and(g != STEP * s % NG, c == 0))
            def _():
                spare_wait.wait_recv()
                spare_copy.start()

            @pl.when(g != STEP * s % NG)
            def _():
                own_copy.wait_recv()

    for s in range(S):
        next_copies = [along_z(s, treesend.at[i], d) for i, d in enumerate((1, -1))]

        @pl.when(z == zero[s])
        def _():
            for cp in next_copies:
                cp.start()

    pl.semaphore_wait(known.at[0], 2)
    wider(1)
    pl.semaphore_wait(known.at[1], 2)
    wider(2)
    for s in range(S):
        hub_copies = [along_z(s, treesend.at[2 + i], d) for i, d in enumerate((4, -4, 2, -2))]

        @pl.when(z == zero[s])
        def _():
            for cp in hub_copies:
                cp.start()

    for s in range(S):
        to_next[s][0].wait_recv()
        far_next[s].start()
        to_prev[s][1].wait_recv()
        far_prev[s].start()
        if s + 1 < S:
            to_next[s + 1][1].start()
            to_prev[s + 1][0].start()

    def place(s, q, pattern, tiles, low, high):
        for i, tile in zip((0, 1, 2, 3, 4, 5, 6, 7), (0, 1, 2, 3, 4, 5, low, high)):
            value = tiles[tile]
            left[pl.ds(i * TILE, TILE), pl.ds(base(s, q), TILE)] = jnp.where(pattern[i] != 0, value, jnp.zeros_like(value))

    for s in range(S):
        place(s, 0, own_pattern[s], own[s], TR - 2, TR - 1)

    rels = [(z - zero[s] + NZ) % NZ for s in range(S)]
    near = [jnp.where(rel % 8 == 4, -1, jnp.minimum(rel, NZ - rel)) for rel in rels]
    closest = jnp.where(jnp.logical_and(near[0] <= near[1], near[0] <= near[2]), 0, jnp.where(near[1] <= near[2], 1, 2))
    farthest = jnp.where(jnp.logical_and(near[2] >= near[0], near[2] >= near[1]), 2, jnp.where(near[1] >= near[0], 1, 0))
    panels = (closest, 3 - closest - farthest, farthest)
    y_copies, c_copies = [], []
    for n, s in enumerate(panels):
        rel = (z - STEP * s // NG + NZ) % NZ
        way = 1 - rel // 8 * 2
        relay_copies = [along_z(s, treesend.at[i], way * d) for i, d in enumerate((4, 3, 2, 1, -1))]

        @pl.when(rel != 0)
        def _():
            along_z(s, treesend.at[0], 4).wait_recv()

        @pl.when(rel == 4 + 8 * c)
        def _():
            relay_copies[0].start()

        @pl.when(rel % 8 == 4)
        def _():
            for cp in relay_copies[1:]:
                cp.start()

        y_copies.append([copy(piece_of(s, g), piece_of(s, g), ysend.at[s, d - 1], yrecv.at[s, d - 1], at_y(d)) for d in range(1, NY)])
        c_copies.append([copy(piece_of(s, (g + NG - 2 * d) % NG), piece_of(s, (g + NG - 2 * d) % NG), csend.at[s, d], crecv.at[s, d], sibling) for d in range(NY)])
        for d in (2, 1, 3):
            y_copies[n][d - 1].start()
        c_copies[n][0].start()

    for cp in pattern_copies:
        cp.wait_recv()

    def received(s, q, tiles):
        pattern = [pats[ORDER[q]][s, 0, i] for i in range(TR)]
        first, last = free_slots(pattern)
        place(s, q, pattern, tiles, first, last)

    for s in range(S):
        to_next[s][1].wait_recv()
        to_prev[s][0].wait_recv()
        received(s, 1, from_next[s])
        received(s, 2, from_prev[s])

    pl.semaphore_wait(known.at[2], 2)

    for s in range(S):
        for d in (1, 3, 2):
            y_copies[s][d - 1].wait_recv()
            c_copies[s][d].start()

    for s in range(S):
        for d in range(NY):
            c_copies[s][d].wait_recv()

    for n in range(2):
        cols = pl.ds(n * 256, 256)
        out[:, cols] = jnp.dot(left[:, :FIRST], right[:FIRST, cols], preferred_element_type=jnp.float32)

    for s in range(S):
        far_next[s].wait_recv()
        far_prev[s].wait_recv()
        received(s, 3, from_far[s])

    for n in range(2):
        cols = pl.ds(n * 256, 256)
        total = out[:, cols] + jnp.dot(left[:, FIRST:], right[FIRST:, cols], preferred_element_type=jnp.float32)
        total = total * total
        out[:, cols] = total
        mine[:, cols] = jnp.sum(total, axis=0, keepdims=True)

    across = copy(mine, other, asend.at[0], arecv.at[0], sibling)
    across.start()
    across.wait_recv()
    pair[...] = mine[...] + other[...]
    a_copies = [copy(pair, chips.at[d - 1], asend.at[d], arecv.at[d], at_y(d)) for d in range(1, NY)]
    for cp in a_copies:
        cp.start()
    for cp in a_copies:
        cp.wait_recv()
    part[...] = pair[...] + jnp.sum(chips[...], axis=0)
    z_copies = [copy(part, column.at[d - 1], zsend.at[d - 1], zrecv.at[d - 1], at_z(d)) for d in range(1, NZ)]
    for d in sorted(range(1, NZ), key=lambda d: -min(d, NZ - d)):
        z_copies[d - 1].start()
    for cp in z_copies:
        cp.wait_recv()
    rows_total = TR * TILE * NZ * NG
    scale[...] = rows_total / (part[...] + jnp.sum(column[...], axis=0))

    @pl.when(is_root)
    def _():
        for cp in root_copies:
            cp.wait_send()

    for s in range(S):
        waiter = [along_z(s, treesend.at[i], 1) for i in range(6)]
        spare_copy = copy(spare, piece_of(s, g + 1 - 2 * c), rootsend.at[6], ownrecv.at[s], sibling)
        rel = rels[s]

        @pl.when(rel == 0)
        def _():
            for cp in waiter:
                cp.wait_send()

        @pl.when(jnp.logical_and(rel == 0, jnp.logical_and(g != STEP * s % NG, c == 0)))
        def _():
            spare_copy.wait_send()

        @pl.when(rel == 4 + 8 * c)
        def _():
            waiter[0].wait_send()

        @pl.when(rel % 8 == 4)
        def _():
            for cp in waiter[1:5]:
                cp.wait_send()

    flat = pattern_copies + far_next + far_prev + [across] + a_copies + z_copies
    for group_of in to_next + to_prev + y_copies + c_copies:
        flat = flat + group_of
    for cp in flat:
        cp.wait_send()


def on_device(left_values, left_pattern, right_values, right_pattern):
    tiles = left_values.reshape(S, TR, TILE, TILE)
    pattern = left_pattern.transpose(0, 2, 1)
    rows = TR * TILE
    dma = pltpu.SemaphoreType.DMA
    box = lambda n: tuple(pltpu.VMEM((n, TILE, TILE), jnp.bfloat16) for _ in range(S))
    any_space, smem, vmem = (pl.BlockSpec(memory_space=m) for m in (pltpu.HBM, pltpu.SMEM, pltpu.VMEM))
    squares, scale = pl.pallas_call(
        kernel,
        out_shape=(pltpu.VMEM((rows, COLS), jnp.float32), pltpu.VMEM((1, COLS), jnp.float32)),
        in_specs=[any_space, smem, any_space, smem],
        out_specs=(vmem, vmem),
        scratch_shapes=[
            box(TR),
            pltpu.VMEM((S, SLOTS, TILE, TILE), jnp.bfloat16),
            box(SLOTS), box(SLOTS), box(SLOTS),
            tuple(pltpu.SMEM((S, 1, TR), jnp.int32) for _ in range(NX)),
            pltpu.VMEM((NX * TILE, COLS), jnp.bfloat16),
            pltpu.VMEM((NX * TILE, COLS), jnp.bfloat16),
            pltpu.VMEM((PIECE, COLS), jnp.bfloat16),
            pltpu.VMEM((rows, S * NX * TILE), jnp.bfloat16),
            pltpu.VMEM((S * NX * TILE, COLS), jnp.bfloat16),
            pltpu.VMEM((1, COLS), jnp.float32),
            pltpu.VMEM((1, COLS), jnp.float32),
            pltpu.VMEM((1, COLS), jnp.float32),
            pltpu.VMEM((NY - 1, 1, COLS), jnp.float32),
            pltpu.VMEM((1, COLS), jnp.float32),
            pltpu.VMEM((NZ - 1, 1, COLS), jnp.float32),
            dma((NX,)), dma((NX,)),
            dma((3, S, 2)), dma((3, S, 2)),
            dma((NG - 1,)), dma((1,)), dma((S,)), dma((6,)),
            dma((S, NY - 1)), dma((S, NY - 1)),
            dma((S, NY)), dma((S, NY)),
            dma((NY,)), dma((NY,)),
            dma((NZ - 1,)), dma((NZ - 1,)),
            dma((S + 1,)),
            pltpu.SemaphoreType.REGULAR((3,)),
        ],
        compiler_params=pltpu.CompilerParams(collective_id=0, has_side_effects=True, vmem_limit_bytes=56 * 1024 * 1024),
    )(*[pltpu.with_memory_space_constraint(a, pltpu.HBM) for a in (tiles, pattern, right_values, right_pattern.T)])
    return squares * scale


def solution(mesh):
    in_specs = (P(None, "row", "col"), P(None, "row", "col"), P("row", "col"), P("row", "col"))
    out_specs = P("row", "col")
    return jax.shard_map(
        on_device, mesh=mesh, in_specs=in_specs, out_specs=out_specs, check_vma=False
    )
```

```python
import jax
import jax.numpy as jnp
from jax import lax
from jax.experimental import pallas as pl
from jax.experimental.pallas import tpu as pltpu
from jax.sharding import PartitionSpec as P

TILE = 128
TR = 8
SLOTS = 6
HALF = SLOTS // 2
S = 3
NX, NZ, NG = 4, 16, 8
NY = 4
STEP = 42
COLS = 512
PIECE = 64
PART = 32
PARTS = PIECE // PART
INNER = NX * TILE
MESH = pl.DeviceIdType.MESH
ORDER = (0, 1, 3, 2)


def base(s, q):
    return s * INNER + q * TILE


def free_slots(pattern):
    first, last = SLOTS - 1, 0
    for i in range(SLOTS):
        last = jnp.where(pattern[i] == 0, i, last)
        first = jnp.where(pattern[SLOTS - 1 - i] == 0, SLOTS - 1 - i, first)
    return first, last


def kernel(left_hbm, pat_hbm, right_hbm, rpat_hbm, out, scale, own, pack, from_next, from_prev, from_far, pat, rpat, pats, raw, root, spare,
           left, right, mine, other, pair, chips, part, column, psend, precv, xsend, xrecv, rootsend, sparerecv, ownrecv, treesend,
           ysend, yrecv, csend, crecv, asend, arecv, zsend, zrecv, load, known):
    r, x = lax.axis_index("row"), lax.axis_index("col")
    z, g = r // NG, r % NG
    y, c = g // 2, g % 2

    def at_x(d):
        return (r, (x + d) % NX)

    def at_z(d):
        return (((z + d + NZ) % NZ) * NG + g, x)

    def at_y(d):
        return (z * NG + ((y + d) % NY) * 2 + c, x)

    sibling = (z * NG + y * 2 + 1 - c, x)

    def copy(src, dst, send, recv, to):
        return pltpu.make_async_remote_copy(src_ref=src, dst_ref=dst, send_sem=send, recv_sem=recv, device_id=to, device_id_type=MESH)

    barrier = pltpu.get_barrier_semaphore()
    peers = [at_x(d) for d in range(1, NX)] + [at_y(d) for d in range(1, NY)] + [sibling] + [at_z(d) for d in (1, NZ - 1)]
    for peer in peers:
        pl.semaphore_signal(barrier, inc=1, device_id=peer, device_id_type=MESH)

    loads = [pltpu.make_async_copy(left_hbm.at[s], own[s], load.at[s]) for s in range(S)]
    load_pattern = pltpu.make_async_copy(pat_hbm, pat, load.at[S + 1])
    load_pattern.start()
    for cp in loads:
        cp.start()
    is_root = jnp.logical_and(r % STEP == 0, r // STEP < S)
    load_right = pltpu.make_async_copy(right_hbm.at[pl.ds(0, NX * TILE)], raw, load.at[S])

    def piece_of(s, p, h):
        return right.at[pl.ds(pl.multiple_of(s * INNER + p * PIECE + h * PART, PART), PART)]

    @pl.when(is_root)
    def _():
        load_right_pattern = pltpu.make_async_copy(rpat_hbm, rpat, load.at[S + 2])
        load_right.start()
        load_right_pattern.start()
        load_right_pattern.wait()
        load_right.wait()
        for q, d in enumerate(ORDER):
            k = (x + d) % NX
            for j in range(COLS // TILE):
                tile = raw[pl.ds(pl.multiple_of(k * TILE, TILE), TILE), pl.ds(j * TILE, TILE)]
                root[pl.ds(q * TILE, TILE), pl.ds(j * TILE, TILE)] = jnp.where(rpat[j, k] != 0, tile, jnp.zeros_like(tile))

    load_pattern.wait()
    own_pattern = [[pat[s, 0, i] for i in range(TR)] for s in range(S)]
    for s in range(S):
        first, last = free_slots(own_pattern[s])
        loads[s].wait()
        for t in range(SLOTS):
            at = jnp.where(jnp.logical_and(own_pattern[s][TR - 2] != 0, first == t), TR - 2, t)
            at = jnp.where(jnp.logical_and(own_pattern[s][TR - 1] != 0, last == t), TR - 1, at)
            pack[s, t] = own[s][at]

    pl.semaphore_wait(barrier, len(peers))

    def wider(step):
        for to in (1 << step, NZ - (1 << step)):
            pl.semaphore_signal(known.at[step], inc=1, device_id=at_z(to), device_id_type=MESH)

    wider(0)

    my_panel = r // STEP

    def of_root(p, h):
        return root.at[pl.ds(pl.multiple_of(p * PIECE + h * PART, PART), PART)]

    spares = [spare.at[pl.ds(h * PART, PART)] for h in range(PARTS)]
    root_copies = []
    for h in range(PARTS):
        for d in (2, 1, 3):
            p = (g + 2 * d) % NG
            root_copies.append(copy(of_root((p + 1) % NG, h), spares[h], rootsend.at[2 * d - 1, h], sparerecv.at[h], at_y(d)))
            root_copies.append(copy(of_root(p, h), piece_of(my_panel, p, h), rootsend.at[2 * d - 2, h], ownrecv.at[my_panel, h], at_y(d)))
        p = g + 1 - 2 * c
        root_copies.append(copy(of_root(p, h), piece_of(my_panel, p, h), rootsend.at[6, h], ownrecv.at[my_panel, h], sibling))

    @pl.when(is_root)
    def _():
        for cp in root_copies:
            cp.start()
        start = pl.multiple_of(my_panel * INNER + g * PIECE, PIECE)
        right[pl.ds(start, PIECE)] = root[pl.ds(pl.multiple_of(g * PIECE, PIECE), PIECE)]

    pattern_copies = [copy(pat, pats[d], psend.at[d], precv.at[d], at_x(NX - d)) for d in range(1, NX)]
    for cp in pattern_copies:
        cp.start()
    halves = [pl.ds(0, HALF), pl.ds(HALF, HALF)]
    to_next = [[copy(pack.at[s, halves[h]], from_prev[s].at[halves[h]], xsend.at[0, s, h], xrecv.at[0, s, h], at_x(1)) for h in range(2)] for s in range(S)]
    to_prev = [[copy(pack.at[s, halves[h]], from_next[s].at[halves[h]], xsend.at[1, s, h], xrecv.at[1, s, h], at_x(NX - 1)) for h in range(2)] for s in range(S)]
    for s, h in ((0, 0), (1, 0), (2, 0), (0, 1)):
        to_next[s][h].start()
        to_prev[s][1 - h].start()
    far_next = [copy(from_prev[s].at[halves[0]], from_far[s].at[halves[0]], xsend.at[2, s, 0], xrecv.at[2, s, 0], at_x(1)) for s in range(S)]
    far_prev = [copy(from_next[s].at[halves[1]], from_far[s].at[halves[1]], xsend.at[2, s, 1], xrecv.at[2, s, 1], at_x(NX - 1)) for s in range(S)]

    def along_z(s, i, d):
        return [copy(piece_of(s, g, h), piece_of(s, g, h), treesend.at[i, h], ownrecv.at[s, h], at_z(d)) for h in range(PARTS)]

    def from_spare(s):
        p = g + 1 - 2 * c
        return [copy(spares[h], piece_of(s, p, h), rootsend.at[6, h], ownrecv.at[s, h], sibling) for h in range(PARTS)]

    zero = [STEP * s // NG for s in range(S)]
    for s in range(S):
        for h in range(PARTS):

            @pl.when(jnp.logical_and(z == zero[s], jnp.logical_and(g != STEP * s % NG, c == 0)))
            def _():
                copy(spares[h], spares[h], rootsend.at[6, h], sparerecv.at[h], sibling).wait_recv()
                from_spare(s)[h].start()

            @pl.when(jnp.logical_and(z == zero[s], g != STEP * s % NG))
            def _():
                along_z(s, 0, 1)[h].wait_recv()

            @pl.when(z == zero[s])
            def _():
                for i, d in enumerate((1, -1)):
                    along_z(s, i, d)[h].start()

    pl.semaphore_wait(known.at[0], 2)
    wider(1)
    pl.semaphore_wait(known.at[1], 2)
    wider(2)
    for s in range(S):

        @pl.when(z == zero[s])
        def _():
            for h in range(PARTS):
                for i, d in enumerate((4, -4)):
                    along_z(s, 2 + i, d)[h].start()
            for h in range(PARTS):
                for i, d in enumerate((2, -2)):
                    along_z(s, 4 + i, d)[h].start()

    for s in range(S):
        to_next[s][0].wait_recv()
        far_next[s].start()
        to_prev[s][1].wait_recv()
        far_prev[s].start()
        if s + 1 < S:
            to_next[s + 1][1].start()
            to_prev[s + 1][0].start()

    def place(s, q, pattern, tiles, low, high):
        for i, tile in zip((0, 1, 2, 3, 4, 5, 6, 7), (0, 1, 2, 3, 4, 5, low, high)):
            value = tiles[tile]
            left[pl.ds(i * TILE, TILE), pl.ds(base(s, q), TILE)] = jnp.where(pattern[i] != 0, value, jnp.zeros_like(value))

    for s in range(S):
        place(s, 0, own_pattern[s], own[s], TR - 2, TR - 1)

    rels = [(z - zero[s] + NZ) % NZ for s in range(S)]
    near = [jnp.where(rel % 8 == 4, -1, jnp.minimum(rel, NZ - rel)) for rel in rels]
    closest = jnp.where(jnp.logical_and(near[0] <= near[1], near[0] <= near[2]), 0, jnp.where(near[1] <= near[2], 1, 2))
    farthest = jnp.where(jnp.logical_and(near[2] >= near[0], near[2] >= near[1]), 2, jnp.where(near[1] >= near[0], 1, 0))
    panels = (closest, 3 - closest - farthest, farthest)
    y_copies, c_copies = [], []
    for n, s in enumerate(panels):
        rel = (z - STEP * s // NG + NZ) % NZ
        way = 1 - rel // 8 * 2
        relay_copies = [along_z(s, i, way * d) for i, d in enumerate((4, 3, 2, 1, -1))]
        sources = [(g + NG - 2 * d) % NG for d in range(NY)]
        y_copies.append([[copy(piece_of(s, g, h), piece_of(s, g, h), ysend.at[s, d - 1, h], yrecv.at[s, d - 1, h], at_y(d)) for d in range(1, NY)] for h in range(PARTS)])
        c_copies.append([[copy(piece_of(s, p, h), piece_of(s, p, h), csend.at[s, d, h], crecv.at[s, d, h], sibling) for d, p in enumerate(sources)] for h in range(PARTS)])
        for h in range(PARTS):

            @pl.when(rel != 0)
            def _():
                along_z(s, 0, 1)[h].wait_recv()

            @pl.when(rel == 4 + 8 * c)
            def _():
                relay_copies[0][h].start()

            @pl.when(rel % 8 == 4)
            def _():
                for cp in relay_copies[1:]:
                    cp[h].start()

            for d in (2, 1, 3):
                y_copies[n][h][d - 1].start()
            c_copies[n][h][0].start()

    for cp in pattern_copies:
        cp.wait_recv()

    def received(s, q, tiles):
        pattern = [pats[ORDER[q]][s, 0, i] for i in range(TR)]
        first, last = free_slots(pattern)
        place(s, q, pattern, tiles, first, last)

    for s in range(S):
        to_next[s][1].wait_recv()
        to_prev[s][0].wait_recv()
        received(s, 1, from_next[s])
        received(s, 2, from_prev[s])

    def to_sibling(n):
        for h in range(PARTS):
            for d in (1, 3, 2):
                y_copies[n][h][d - 1].wait_recv()
                c_copies[n][h][d].start()

    to_sibling(0)
    to_sibling(1)
    for s in range(S):
        far_next[s].wait_recv()
        far_prev[s].wait_recv()
        received(s, 3, from_far[s])
    pl.semaphore_wait(known.at[2], 2)
    to_sibling(2)

    for n, s in enumerate(panels):
        for h in range(PARTS):
            for d in range(NY):
                c_copies[n][h][d].wait_recv()
        inner = pl.ds(pl.multiple_of(s * INNER, INNER), INNER)
        for b in range(2):
            cols = pl.ds(b * 256, 256)
            total = jnp.dot(left[:, inner], right[inner, cols], preferred_element_type=jnp.float32)
            if n > 0:
                total = total + out[:, cols]
            if n == S - 1:
                total = total * total
                mine[:, cols] = jnp.sum(total, axis=0, keepdims=True)
            out[:, cols] = total

    across = copy(mine, other, asend.at[0], arecv.at[0], sibling)
    across.start()
    across.wait_recv()
    pair[...] = mine[...] + other[...]
    a_copies = [copy(pair, chips.at[d - 1], asend.at[d], arecv.at[d], at_y(d)) for d in range(1, NY)]
    for cp in a_copies:
        cp.start()
    for cp in a_copies:
        cp.wait_recv()
    part[...] = pair[...] + jnp.sum(chips[...], axis=0)
    z_copies = [copy(part, column.at[d - 1], zsend.at[d - 1], zrecv.at[d - 1], at_z(d)) for d in range(1, NZ)]
    for d in sorted(range(1, NZ), key=lambda d: -min(d, NZ - d)):
        z_copies[d - 1].start()
    for cp in z_copies:
        cp.wait_recv()
    rows_total = TR * TILE * NZ * NG
    scale[...] = rows_total / (part[...] + jnp.sum(column[...], axis=0))

    @pl.when(is_root)
    def _():
        for cp in root_copies:
            cp.wait_send()

    for s in range(S):
        rel = rels[s]
        for h in range(PARTS):

            @pl.when(rel == 0)
            def _():
                for i in range(6):
                    along_z(s, i, 1)[h].wait_send()

            @pl.when(jnp.logical_and(rel == 0, jnp.logical_and(g != STEP * s % NG, c == 0)))
            def _():
                from_spare(s)[h].wait_send()

            @pl.when(rel == 4 + 8 * c)
            def _():
                along_z(s, 0, 1)[h].wait_send()

            @pl.when(rel % 8 == 4)
            def _():
                for i in range(1, 5):
                    along_z(s, i, 1)[h].wait_send()

    flat = pattern_copies + far_next + far_prev + [across] + a_copies + z_copies
    for group_of in to_next + to_prev:
        flat = flat + group_of
    for panel in y_copies + c_copies:
        for group_of in panel:
            flat = flat + group_of
    for cp in flat:
        cp.wait_send()


def on_device(left_values, left_pattern, right_values, right_pattern):
    tiles = left_values.reshape(S, TR, TILE, TILE)
    pattern = left_pattern.transpose(0, 2, 1)
    rows = TR * TILE
    dma = pltpu.SemaphoreType.DMA
    box = lambda n: tuple(pltpu.VMEM((n, TILE, TILE), jnp.bfloat16) for _ in range(S))
    hbm, vmem = (pl.BlockSpec(memory_space=m) for m in (pltpu.HBM, pltpu.VMEM))
    squares, scale = pl.pallas_call(
        kernel,
        out_shape=(pltpu.VMEM((rows, COLS), jnp.float32), pltpu.VMEM((1, COLS), jnp.float32)),
        in_specs=[hbm] * 4,
        out_specs=(vmem, vmem),
        scratch_shapes=[
            box(TR),
            pltpu.VMEM((S, SLOTS, TILE, TILE), jnp.bfloat16),
            box(SLOTS), box(SLOTS), box(SLOTS),
            pltpu.SMEM((S, 1, TR), jnp.int32),
            pltpu.SMEM((COLS // TILE, TR), jnp.int32),
            tuple(pltpu.SMEM((S, 1, TR), jnp.int32) for _ in range(NX)),
            pltpu.VMEM((NX * TILE, COLS), jnp.bfloat16),
            pltpu.VMEM((NX * TILE, COLS), jnp.bfloat16),
            pltpu.VMEM((PIECE, COLS), jnp.bfloat16),
            pltpu.VMEM((rows, S * NX * TILE), jnp.bfloat16),
            pltpu.VMEM((S * NX * TILE, COLS), jnp.bfloat16),
            pltpu.VMEM((1, COLS), jnp.float32),
            pltpu.VMEM((1, COLS), jnp.float32),
            pltpu.VMEM((1, COLS), jnp.float32),
            pltpu.VMEM((NY - 1, 1, COLS), jnp.float32),
            pltpu.VMEM((1, COLS), jnp.float32),
            pltpu.VMEM((NZ - 1, 1, COLS), jnp.float32),
            dma((NX,)), dma((NX,)),
            dma((3, S, 2)), dma((3, S, 2)),
            dma((NG - 1, PARTS)), dma((PARTS,)), dma((S, PARTS)), dma((6, PARTS)),
            dma((S, NY - 1, PARTS)), dma((S, NY - 1, PARTS)),
            dma((S, NY, PARTS)), dma((S, NY, PARTS)),
            dma((NY,)), dma((NY,)),
            dma((NZ - 1,)), dma((NZ - 1,)),
            dma((S + 3,)),
            pltpu.SemaphoreType.REGULAR((3,)),
        ],
        compiler_params=pltpu.CompilerParams(collective_id=0, has_side_effects=True, vmem_limit_bytes=56 * 1024 * 1024),
    )(*[pltpu.with_memory_space_constraint(a, pltpu.HBM) for a in (tiles, pattern, right_values, right_pattern.T)])
    return squares * scale


def solution(mesh):
    in_specs = (P(None, "row", "col"), P(None, "row", "col"), P("row", "col"), P("row", "col"))
    out_specs = P("row", "col")
    return jax.shard_map(
        on_device, mesh=mesh, in_specs=in_specs, out_specs=out_specs, check_vma=False
    )
```

```python
import jax
import jax.numpy as jnp
from jax import lax
from jax.experimental import pallas as pl
from jax.experimental.pallas import tpu as pltpu
from jax.sharding import PartitionSpec as P

TILE = 128
TR = 8
SLOTS = 6
HALF = SLOTS // 2
S = 3
NX, NZ, NG = 4, 16, 8
NY = 4
STEP = 42
COLS = 512
PIECE = 64
PART = 32
PARTS = PIECE // PART
INNER = NX * TILE
MESH = pl.DeviceIdType.MESH
ORDER = (0, 1, 3, 2)


def base(s, q):
    return s * INNER + q * TILE


def free_slots(pattern):
    first, last = SLOTS - 1, 0
    for i in range(SLOTS):
        last = jnp.where(pattern[i] == 0, i, last)
        first = jnp.where(pattern[SLOTS - 1 - i] == 0, SLOTS - 1 - i, first)
    return first, last


def kernel(left_hbm, pat_hbm, right_hbm, rpat_hbm, out, scale, own, pack, from_next, from_prev, from_far, pat, rpat, pats, raw, root, spare,
           left, right, mine, other, pair, chips, part, column, psend, precv, xsend, xrecv, rootsend, sparerecv, ownrecv, treesend,
           ysend, yrecv, csend, crecv, asend, arecv, zsend, zrecv, load, known):
    r, x = lax.axis_index("row"), lax.axis_index("col")
    z, g = r // NG, r % NG
    y, c = g // 2, g % 2

    def at_x(d):
        return (r, (x + d) % NX)

    def at_z(d):
        return (((z + d + NZ) % NZ) * NG + g, x)

    def at_y(d):
        return (z * NG + ((y + d) % NY) * 2 + c, x)

    sibling = (z * NG + y * 2 + 1 - c, x)

    def copy(src, dst, send, recv, to):
        return pltpu.make_async_remote_copy(src_ref=src, dst_ref=dst, send_sem=send, recv_sem=recv, device_id=to, device_id_type=MESH)

    barrier = pltpu.get_barrier_semaphore()
    peers = [at_x(d) for d in range(1, NX)] + [at_y(d) for d in range(1, NY)] + [sibling] + [at_z(d) for d in (1, NZ - 1)]
    for peer in peers:
        pl.semaphore_signal(barrier, inc=1, device_id=peer, device_id_type=MESH)

    loads = [pltpu.make_async_copy(left_hbm.at[s], own[s], load.at[s]) for s in range(S)]
    load_pattern = pltpu.make_async_copy(pat_hbm, pat, load.at[S + 1])
    load_pattern.start()
    for cp in loads:
        cp.start()
    is_root = jnp.logical_and(r % STEP == 0, r // STEP < S)
    load_right = pltpu.make_async_copy(right_hbm.at[pl.ds(0, NX * TILE)], raw, load.at[S])

    def piece_of(s, p, h):
        return right.at[pl.ds(pl.multiple_of(s * INNER + p * PIECE + h * PART, PART), PART)]

    @pl.when(is_root)
    def _():
        load_right_pattern = pltpu.make_async_copy(rpat_hbm, rpat, load.at[S + 2])
        load_right.start()
        load_right_pattern.start()
        load_right_pattern.wait()
        load_right.wait()
        for q, d in enumerate(ORDER):
            k = (x + d) % NX
            for j in range(COLS // TILE):
                tile = raw[pl.ds(pl.multiple_of(k * TILE, TILE), TILE), pl.ds(j * TILE, TILE)]
                root[pl.ds(q * TILE, TILE), pl.ds(j * TILE, TILE)] = jnp.where(rpat[j, k] != 0, tile, jnp.zeros_like(tile))

    load_pattern.wait()
    own_pattern = [[pat[s, 0, i] for i in range(TR)] for s in range(S)]
    for s in range(S):
        first, last = free_slots(own_pattern[s])
        loads[s].wait()
        for t in range(SLOTS):
            at = jnp.where(jnp.logical_and(own_pattern[s][TR - 2] != 0, first == t), TR - 2, t)
            at = jnp.where(jnp.logical_and(own_pattern[s][TR - 1] != 0, last == t), TR - 1, at)
            pack[s, t] = own[s][at]

    pl.semaphore_wait(barrier, len(peers))

    def wider(step):
        for to in (1 << step, NZ - (1 << step)):
            pl.semaphore_signal(known.at[step], inc=1, device_id=at_z(to), device_id_type=MESH)

    wider(0)

    my_panel = r // STEP

    def of_root(p, h):
        return root.at[pl.ds(pl.multiple_of(p * PIECE + h * PART, PART), PART)]

    spares = [spare.at[pl.ds(h * PART, PART)] for h in range(PARTS)]
    root_copies = []
    for h in range(PARTS):
        for d in (2, 1, 3):
            p = (g + 2 * d) % NG
            root_copies.append(copy(of_root((p + 1) % NG, h), spares[h], rootsend.at[2 * d - 1, h], sparerecv.at[h], at_y(d)))
            root_copies.append(copy(of_root(p, h), piece_of(my_panel, p, h), rootsend.at[2 * d - 2, h], ownrecv.at[my_panel, h], at_y(d)))
        p = g + 1 - 2 * c
        root_copies.append(copy(of_root(p, h), piece_of(my_panel, p, h), rootsend.at[6, h], ownrecv.at[my_panel, h], sibling))

    @pl.when(is_root)
    def _():
        for cp in root_copies:
            cp.start()
        start = pl.multiple_of(my_panel * INNER + g * PIECE, PIECE)
        right[pl.ds(start, PIECE)] = root[pl.ds(pl.multiple_of(g * PIECE, PIECE), PIECE)]

    pattern_copies = [copy(pat, pats[d], psend.at[d], precv.at[d], at_x(NX - d)) for d in range(1, NX)]
    for cp in pattern_copies:
        cp.start()
    halves = [pl.ds(0, HALF), pl.ds(HALF, HALF)]
    to_next = [[copy(pack.at[s, halves[h]], from_prev[s].at[halves[h]], xsend.at[0, s, h], xrecv.at[0, s, h], at_x(1)) for h in range(2)] for s in range(S)]
    to_prev = [[copy(pack.at[s, halves[h]], from_next[s].at[halves[h]], xsend.at[1, s, h], xrecv.at[1, s, h], at_x(NX - 1)) for h in range(2)] for s in range(S)]
    for s, h in ((0, 0), (1, 0), (2, 0), (0, 1)):
        to_next[s][h].start()
        to_prev[s][1 - h].start()
    far_next = [copy(from_prev[s].at[halves[0]], from_far[s].at[halves[0]], xsend.at[2, s, 0], xrecv.at[2, s, 0], at_x(1)) for s in range(S)]
    far_prev = [copy(from_next[s].at[halves[1]], from_far[s].at[halves[1]], xsend.at[2, s, 1], xrecv.at[2, s, 1], at_x(NX - 1)) for s in range(S)]

    def along_z(s, i, d):
        return [copy(piece_of(s, g, h), piece_of(s, g, h), treesend.at[i, h], ownrecv.at[s, h], at_z(d)) for h in range(PARTS)]

    def from_spare(s):
        p = g + 1 - 2 * c
        return [copy(spares[h], piece_of(s, p, h), rootsend.at[6, h], ownrecv.at[s, h], sibling) for h in range(PARTS)]

    zero = [STEP * s // NG for s in range(S)]
    for s in range(S):
        for h in range(PARTS):

            @pl.when(jnp.logical_and(z == zero[s], jnp.logical_and(g != STEP * s % NG, c == 0)))
            def _():
                copy(spares[h], spares[h], rootsend.at[6, h], sparerecv.at[h], sibling).wait_recv()
                from_spare(s)[h].start()

            @pl.when(jnp.logical_and(z == zero[s], g != STEP * s % NG))
            def _():
                along_z(s, 0, 1)[h].wait_recv()

            @pl.when(z == zero[s])
            def _():
                for i, d in enumerate((1, -1)):
                    along_z(s, i, d)[h].start()

    pl.semaphore_wait(known.at[0], 2)
    wider(1)
    pl.semaphore_wait(known.at[1], 2)
    wider(2)
    for s in range(S):

        @pl.when(z == zero[s])
        def _():
            for h in range(PARTS):
                for i, d in enumerate((4, -4)):
                    along_z(s, 2 + i, d)[h].start()

    for s in range(S):
        to_next[s][0].wait_recv()
        far_next[s].start()
        to_prev[s][1].wait_recv()
        far_prev[s].start()
        if s + 1 < S:
            to_next[s + 1][1].start()
            to_prev[s + 1][0].start()

    def place(s, q, pattern, tiles, low, high):
        for i, tile in zip((0, 1, 2, 3, 4, 5, 6, 7), (0, 1, 2, 3, 4, 5, low, high)):
            value = tiles[tile]
            left[pl.ds(i * TILE, TILE), pl.ds(base(s, q), TILE)] = jnp.where(pattern[i] != 0, value, jnp.zeros_like(value))

    for s in range(S):
        place(s, 0, own_pattern[s], own[s], TR - 2, TR - 1)

    rels = [(z - zero[s] + NZ) % NZ for s in range(S)]
    near = [jnp.where(rel % 8 == 4, -1, jnp.minimum(rel, NZ - rel)) for rel in rels]
    closest = jnp.where(jnp.logical_and(near[0] <= near[1], near[0] <= near[2]), 0, jnp.where(near[1] <= near[2], 1, 2))
    farthest = jnp.where(jnp.logical_and(near[2] >= near[0], near[2] >= near[1]), 2, jnp.where(near[1] >= near[0], 1, 0))
    panels = (closest, 3 - closest - farthest, farthest)
    y_copies, c_copies = [], []
    for n, s in enumerate(panels):
        rel = (z - STEP * s // NG + NZ) % NZ
        way = 1 - rel // 8 * 2
        relay_copies = [along_z(s, i, way * d) for i, d in enumerate((4, 3, 2, 1, -1))]
        sources = [(g + NG - 2 * d) % NG for d in range(NY)]
        y_copies.append([[copy(piece_of(s, g, h), piece_of(s, g, h), ysend.at[s, d - 1, h], yrecv.at[s, d - 1, h], at_y(d)) for d in range(1, NY)] for h in range(PARTS)])
        c_copies.append([[copy(piece_of(s, p, h), piece_of(s, p, h), csend.at[s, d, h], crecv.at[s, d, h], sibling) for d, p in enumerate(sources)] for h in range(PARTS)])
        for h in range(PARTS):

            @pl.when(rel != 0)
            def _():
                along_z(s, 0, 1)[h].wait_recv()

            @pl.when(rel == 4 + 8 * c)
            def _():
                relay_copies[0][h].start()

            @pl.when(rel % 8 == 4)
            def _():
                for cp in relay_copies[1:]:
                    cp[h].start()

            for d in (2, 1, 3):
                y_copies[n][h][d - 1].start()
            c_copies[n][h][0].start()

        @pl.when(rel == 0)
        def _():
            for i, d in enumerate((2, -2)):
                for cp in along_z(s, 4 + i, d):
                    cp.start()

    for cp in pattern_copies:
        cp.wait_recv()

    def received(s, q, tiles):
        pattern = [pats[ORDER[q]][s, 0, i] for i in range(TR)]
        first, last = free_slots(pattern)
        place(s, q, pattern, tiles, first, last)

    for s in range(S):
        to_next[s][1].wait_recv()
        to_prev[s][0].wait_recv()
        received(s, 1, from_next[s])
        received(s, 2, from_prev[s])

    def to_sibling(n):
        for h in range(PARTS):
            for d in (1, 3, 2):
                y_copies[n][h][d - 1].wait_recv()
                c_copies[n][h][d].start()

    to_sibling(0)
    to_sibling(1)
    for s in range(S):
        far_next[s].wait_recv()
        far_prev[s].wait_recv()
        received(s, 3, from_far[s])
    pl.semaphore_wait(known.at[2], 2)
    to_sibling(2)

    for n, s in enumerate(panels):
        for h in range(PARTS):
            for d in range(NY):
                c_copies[n][h][d].wait_recv()
        inner = pl.ds(pl.multiple_of(s * INNER, INNER), INNER)
        for b in range(2):
            cols = pl.ds(b * 256, 256)
            total = jnp.dot(left[:, inner], right[inner, cols], preferred_element_type=jnp.float32)
            if n > 0:
                total = total + out[:, cols]
            if n == S - 1:
                total = total * total
                mine[:, cols] = jnp.sum(total, axis=0, keepdims=True)
            out[:, cols] = total

    across = copy(mine, other, asend.at[0], arecv.at[0], sibling)
    across.start()
    across.wait_recv()
    pair[...] = mine[...] + other[...]
    a_copies = [copy(pair, chips.at[d - 1], asend.at[d], arecv.at[d], at_y(d)) for d in range(1, NY)]
    for cp in a_copies:
        cp.start()
    for cp in a_copies:
        cp.wait_recv()
    part[...] = pair[...] + jnp.sum(chips[...], axis=0)
    z_copies = [copy(part, column.at[d - 1], zsend.at[d - 1], zrecv.at[d - 1], at_z(d)) for d in range(1, NZ)]
    for d in sorted(range(1, NZ), key=lambda d: -min(d, NZ - d)):
        z_copies[d - 1].start()
    for cp in z_copies:
        cp.wait_recv()
    rows_total = TR * TILE * NZ * NG
    scale[...] = rows_total / (part[...] + jnp.sum(column[...], axis=0))

    @pl.when(is_root)
    def _():
        for cp in root_copies:
            cp.wait_send()

    for s in range(S):
        rel = rels[s]
        for h in range(PARTS):

            @pl.when(rel == 0)
            def _():
                for i in range(6):
                    along_z(s, i, 1)[h].wait_send()

            @pl.when(jnp.logical_and(rel == 0, jnp.logical_and(g != STEP * s % NG, c == 0)))
            def _():
                from_spare(s)[h].wait_send()

            @pl.when(rel == 4 + 8 * c)
            def _():
                along_z(s, 0, 1)[h].wait_send()

            @pl.when(rel % 8 == 4)
            def _():
                for i in range(1, 5):
                    along_z(s, i, 1)[h].wait_send()

    flat = pattern_copies + far_next + far_prev + [across] + a_copies + z_copies
    for group_of in to_next + to_prev:
        flat = flat + group_of
    for panel in y_copies + c_copies:
        for group_of in panel:
            flat = flat + group_of
    for cp in flat:
        cp.wait_send()


def on_device(left_values, left_pattern, right_values, right_pattern):
    tiles = left_values.reshape(S, TR, TILE, TILE)
    pattern = left_pattern.transpose(0, 2, 1)
    rows = TR * TILE
    dma = pltpu.SemaphoreType.DMA
    box = lambda n: tuple(pltpu.VMEM((n, TILE, TILE), jnp.bfloat16) for _ in range(S))
    hbm, vmem = (pl.BlockSpec(memory_space=m) for m in (pltpu.HBM, pltpu.VMEM))
    squares, scale = pl.pallas_call(
        kernel,
        out_shape=(pltpu.VMEM((rows, COLS), jnp.float32), pltpu.VMEM((1, COLS), jnp.float32)),
        in_specs=[hbm] * 4,
        out_specs=(vmem, vmem),
        scratch_shapes=[
            box(TR),
            pltpu.VMEM((S, SLOTS, TILE, TILE), jnp.bfloat16),
            box(SLOTS), box(SLOTS), box(SLOTS),
            pltpu.SMEM((S, 1, TR), jnp.int32),
            pltpu.SMEM((COLS // TILE, TR), jnp.int32),
            tuple(pltpu.SMEM((S, 1, TR), jnp.int32) for _ in range(NX)),
            pltpu.VMEM((NX * TILE, COLS), jnp.bfloat16),
            pltpu.VMEM((NX * TILE, COLS), jnp.bfloat16),
            pltpu.VMEM((PIECE, COLS), jnp.bfloat16),
            pltpu.VMEM((rows, S * NX * TILE), jnp.bfloat16),
            pltpu.VMEM((S * NX * TILE, COLS), jnp.bfloat16),
            pltpu.VMEM((1, COLS), jnp.float32),
            pltpu.VMEM((1, COLS), jnp.float32),
            pltpu.VMEM((1, COLS), jnp.float32),
            pltpu.VMEM((NY - 1, 1, COLS), jnp.float32),
            pltpu.VMEM((1, COLS), jnp.float32),
            pltpu.VMEM((NZ - 1, 1, COLS), jnp.float32),
            dma((NX,)), dma((NX,)),
            dma((3, S, 2)), dma((3, S, 2)),
            dma((NG - 1, PARTS)), dma((PARTS,)), dma((S, PARTS)), dma((6, PARTS)),
            dma((S, NY - 1, PARTS)), dma((S, NY - 1, PARTS)),
            dma((S, NY, PARTS)), dma((S, NY, PARTS)),
            dma((NY,)), dma((NY,)),
            dma((NZ - 1,)), dma((NZ - 1,)),
            dma((S + 3,)),
            pltpu.SemaphoreType.REGULAR((3,)),
        ],
        compiler_params=pltpu.CompilerParams(collective_id=0, has_side_effects=True, vmem_limit_bytes=56 * 1024 * 1024),
    )(*[pltpu.with_memory_space_constraint(a, pltpu.HBM) for a in (tiles, pattern, right_values, right_pattern.T)])
    return squares * scale


def solution(mesh):
    in_specs = (P(None, "row", "col"), P(None, "row", "col"), P("row", "col"), P("row", "col"))
    out_specs = P("row", "col")
    return jax.shard_map(
        on_device, mesh=mesh, in_specs=in_specs, out_specs=out_specs, check_vma=False
    )
```
